512 devices in a mesh: row: 32 (over y, z_lo), col: 16 (over x, z_hi, core).
Axes of the slice: x: 4, y: 8, z: 8 (z_hi: 2, z_lo: 4; z = z_hi * 4 + z_lo), core: 2. Of those that a mesh axis runs over, the one named last changes fastest.
Arguments:
- density: float32 [32, 32, 4, 128, 128], P('row', 'col'), as said below
- pattern: int32 [32, 32, 4], P('row', 'col'), may hold values from 0 to 8, as said below
- retained: int32 [32, 32, 4], P('row', 'col'), may hold values from 0 to 8, as said below
Outputs:
- purified: float32 [32, 32, 4, 128, 128], P('row', 'col')
The draws below stay inside these ranges and needn't reach their ends.
Inputs may be any that keep to these rules, and one draw needn't show every extreme that they name: Slot 0 of every block row holds code 4, the site itself; the 4 codes of a block row are distinct; the pattern is symmetric: x holds c exactly when x + offset(c) holds 8 - c. `retained`: slot 0 of every block row holds code 4, the site itself; the 4 codes of a block row are distinct; the pattern is symmetric: x holds c exactly when x + offset(c) holds 8 - c. `density`: the matrix is symmetric: the block of x on code c is the transpose of the block of x + offset(c) on code 8 - c, and every block on code 4 is symmetric.
All inputs are finite; a program needn't handle non-finite values.
Results may differ from the reference program's by a relative error of at most 0.0003.
Values sent between devices are 32-bit elements; how exact they have to be, the bound alone decides.
No kernel may reach another device: no remote copies, remote signals or barrier semaphores. Data moves between devices by JAX's collectives and lax.ppermute only.
A program may use at most 64 MiB of HBM per device.

```python
import jax
import jax.numpy as jnp
from jax import lax

BLOCK = 128
SLOTS = 4
STEPS = 2
SITES_A = 32
SITES_B = 32


def draw_codes(key):
    axis_key = jax.random.fold_in(key, 1)
    parity_a_key = jax.random.fold_in(key, 3)
    parity_b_key = jax.random.fold_in(key, 4)
    order_key = jax.random.fold_in(key, 5)
    matched_axis = jax.random.randint(axis_key, (), 0, 2, dtype=jnp.int32)
    parity_cols = jax.random.randint(parity_a_key, (SITES_B,), 0, 2, dtype=jnp.int32)
    parity_rows = jax.random.randint(parity_b_key, (SITES_A,), 0, 2, dtype=jnp.int32)
    grid_a = jnp.arange(SITES_A, dtype=jnp.int32)[:, None]
    grid_b = jnp.arange(SITES_B, dtype=jnp.int32)[None, :]
    match_first = jnp.where((grid_a + parity_cols[None, :]) % 2 == 0, 7, 1)
    match_second = jnp.where((grid_b + parity_rows[:, None]) % 2 == 0, 5, 3)
    matched = jnp.where(matched_axis == 0, match_first, match_second).astype(jnp.int32)
    lower = jnp.zeros((SITES_A, SITES_B), jnp.int32)
    upper = (8 - lower).astype(jnp.int32)
    three = jnp.stack([lower, upper, matched], axis=2)
    shuffled = jax.random.permutation(order_key, three, axis=2, independent=True)
    own_code = jnp.full((SITES_A, SITES_B, 1), 4, jnp.int32)
    return jnp.concatenate([own_code, shuffled], axis=2)


def draw_pattern(key, part):
    return draw_codes(jax.random.fold_in(key, 11))


def draw_retained(key, part):
    return draw_codes(jax.random.fold_in(key, 23))


def draw_noise(noise_key, shape):
    return jax.random.normal(noise_key, shape, jnp.float32) * 0.015


def draw_density(key, part):
    codes = draw_codes(jax.random.fold_in(key, 11))
    base_key = jax.random.fold_in(key, 37)
    self_key = jax.random.fold_in(key, 43)
    level_key = jax.random.fold_in(key, 41)
    base = draw_noise(base_key, (SITES_A, SITES_B, 4, BLOCK, BLOCK))
    raw_self = draw_noise(self_key, (SITES_A, SITES_B, BLOCK, BLOCK))
    levels = jax.random.uniform(level_key, (SITES_A, SITES_B, BLOCK), jnp.float32, 0.1, 0.9)
    identity = jnp.eye(BLOCK, dtype=jnp.float32)
    self_block = (raw_self + jnp.swapaxes(raw_self, 2, 3)) * 0.70710678 + levels[:, :, :, None] * identity[None, None, :, :]
    slots = []
    for slot_idx in range(SLOTS):
        code_here = codes[:, :, slot_idx][:, :, None, None]
        chosen = jnp.where(code_here == 4, self_block, 0.0)
        for code_low in range(4):
            chosen = jnp.where(code_here == code_low, base[:, :, code_low], chosen)
            code_high = 8 - code_low
            shift_a = code_high // 3 - 1
            shift_b = code_high % 3 - 1
            moved = jnp.roll(base[:, :, code_low], (-shift_a, -shift_b), axis=(0, 1))
            chosen = jnp.where(code_here == code_high, jnp.swapaxes(moved, 2, 3), chosen)
        slots.append(chosen)
    return jnp.stack(slots, axis=2)


def setup_inputs(seed: int = 0) -> dict:
    key_list = jax.random.split(jax.random.key(seed), 4)
    return {
        "density": draw_density(jax.random.fold_in(key_list[3], 71), 0),
        "pattern": draw_pattern(jax.random.fold_in(key_list[3], 71), 0),
        "retained": draw_retained(jax.random.fold_in(key_list[3], 71), 0),
    }


def offsets(codes):
    return codes // 3 - 1, codes % 3 - 1


def multiply(left_blocks, left_codes, right_blocks, right_codes, out_codes):
    lattice_a = left_codes.shape[0]
    lattice_b = left_codes.shape[1]
    slot_count = left_codes.shape[2]
    columns_b = jnp.arange(lattice_b, dtype=jnp.int32)
    out_a, out_b = offsets(out_codes)

    def one_row(index_a):
        row_blocks = left_blocks[index_a]
        row_codes = left_codes[index_a]
        row_out_a = out_a[index_a]
        row_out_b = out_b[index_a]
        summed = jnp.zeros(row_blocks.shape, jnp.float32)
        for slot_idx in range(slot_count):
            step_a, step_b = offsets(row_codes[:, slot_idx])
            near_a = ((index_a + step_a) % lattice_a).astype(jnp.int32)
            near_b = ((columns_b + step_b) % lattice_b).astype(jnp.int32)
            near_blocks = right_blocks[near_a, near_b]
            their_a, their_b = offsets(right_codes[near_a, near_b])
            reach_a = step_a[:, None] + their_a
            reach_b = step_b[:, None] + their_b
            matches = ((reach_a[:, :, None] == row_out_a[:, None, :]) & (reach_b[:, :, None] == row_out_b[:, None, :])).astype(jnp.float32)
            products = jnp.einsum("xij,xtjk->xtik", row_blocks[:, slot_idx], near_blocks, precision=lax.Precision.HIGHEST)
            summed = summed + jnp.einsum("xtu,xtik->xuik", matches, products, precision=lax.Precision.HIGHEST)
        return summed

    return lax.map(one_row, jnp.arange(lattice_a, dtype=jnp.int32))


def reference(density, pattern, retained):
    iterate = density
    codes = pattern
    for iteration in range(STEPS):
        square = multiply(iterate, codes, iterate, codes, retained)
        cubed = multiply(square, retained, iterate, codes, retained)
        iterate = 3.0 * square - 2.0 * cubed
        codes = retained
    return iterate
```

```python
import jax
import jax.numpy as jnp
import numpy as np
from jax import lax
from jax.experimental import pallas as pl
from jax.experimental.pallas import tpu as pltpu
from jax.sharding import PartitionSpec as P

N = 128
SLOTS = 4
TILE = 8
VROWS = 7 * N + TILE
HROWS = TILE + 3 * N


OWN, BELOW, ABOVE, LEFT, RIGHT, CORNER, ZERO, T0 = 0, 8, 15, 22, 25, 28, 32, 33
STEP1_BLOCKS = 65


def ring_table():
    m = np.full((12, 9), ZERO, np.int32)
    for p, b in ((9, 28), (9, 8), (8, 28), (11, 29), (0, 30), (3, 31)):
        m[p, 4] = b
    m[9, 4], m[10, 4], m[1, 4], m[2, 4] = BELOW, BELOW + 1, ABOVE, ABOVE + 1
    m[4, 4], m[7, 4] = LEFT, RIGHT

    def edge(p, code, block):
        m[p, code] = block
        m[p + (code // 3 - 1) * 4 + code % 3 - 1, 8 - code] = T0 + block

    for base, p, left, right in ((BELOW, 9, 0, 2), (ABOVE, 1, 6, 8)):
        edge(p, 5, base + 2)
        edge(p, 3, base + 3)
        edge(p + 1, 5, base + 4)
        edge(p, left, base + 5)
        edge(p + 1, right, base + 6)
    for base, p in ((LEFT, 4), (RIGHT, 7)):
        edge(p, 1, base + 1)
        edge(p, 7, base + 2)
    return m.reshape(-1)


TURNED = [s for s in range(1, 4)] + [4 + s for s in range(1, 4)]
TURNED += [b + i for b in (BELOW, ABOVE) for i in range(2, 7)]
TURNED += [b + i for b in (LEFT, RIGHT) for i in (1, 2)]

FAR_TABLE = np.zeros((2, 12, 2), np.int32)
for parity in range(2):
    far, near = (0, 3) if parity == 0 else (3, 0)
    for x in range(2):
        pos = x ^ parity
        FAR_TABLE[parity, 5 + x] = 40 + 4 * x, 4 * pos
        FAR_TABLE[parity, 9 + x] = 4 * x, 8 + 4 * pos
        FAR_TABLE[parity, 1 + x] = 8 + 4 * x, 16 + 4 * pos
    FAR_TABLE[parity, 4 + far] = 16, 24
    FAR_TABLE[parity, 4 + near] = 20, 28
    FAR_TABLE[parity, 8 + far] = 24, 32
    FAR_TABLE[parity, 8 + near] = 28, 44
    FAR_TABLE[parity, 0 + far] = 32, 36
    FAR_TABLE[parity, 0 + near] = 36, 40
STEP2_ZERO = 48
STEP2_BLOCKS = 49


def rows_of(block, count=1):
    if isinstance(block, int):
        return pl.ds(block * N, count * N)
    return pl.ds(pl.multiple_of(block * N, N), count * N)


def offset(code):
    return lax.div(code, 3) - 1, lax.rem(code, 3) - 1


def relative(left, out):
    la, lb = offset(left)
    oa, ob = offset(out)
    a, b = oa - la, ob - lb
    near = (a >= -1) & (a <= 1) & (b >= -1) & (b <= 1)
    return (a + 1) * 3 + b + 1, near


def halves(value):
    high = value.astype(jnp.bfloat16)
    return high, (value - high.astype(jnp.float32)).astype(jnp.bfloat16)


def put_factor(buf, where, high_ref, low_ref, s, u):
    high, low = halves(buf[rows_of(where), :])
    at = (pl.ds(s * N, N), pl.ds(u * N, N))
    high_ref[at] = high
    low_ref[at] = low


def times(left, high_ref, low_ref):
    high, low = halves(left)
    both = jnp.dot(jnp.concatenate([high, low], axis=0), high_ref[...], preferred_element_type=jnp.float32)
    return both[:N] + both[N:] + jnp.dot(high, low_ref[...], preferred_element_type=jnp.float32)


def code_tile(codes, start, count):
    lane = lax.broadcasted_iota(jnp.int32, (TILE, N), 1)
    tile = jnp.zeros((TILE, N), jnp.float32)
    for j in range(count):
        tile = jnp.where(lane == j, codes[start + j].astype(jnp.float32), tile)
    return tile


def pack_kernel(pattern, retained, parity, density, up, down, far, near):
    def find(x, code):
        slot = jnp.int32(-1)
        for t in range(SLOTS):
            slot = jnp.where(pattern[SLOTS * x + t] == code, SLOTS * x + t, slot)
        return slot

    def place(slot, targets):
        block = density[rows_of(jnp.maximum(slot, 0)), :] * (slot >= 0).astype(jnp.float32)
        for ref, first in targets:
            ref[pl.ds(first, N), :] = block

    for i, (x, code) in enumerate(((0, 4), (1, 4), (0, 5), (0, 3), (1, 5))):
        place(find(x, code), ((up, i * N), (down, i * N)))
    place(find(0, 0), ((up, 5 * N),))
    place(find(1, 2), ((up, 6 * N),))
    place(find(0, 6), ((down, 5 * N),))
    place(find(1, 8), ((down, 6 * N),))
    tile = code_tile(retained, 0, 2 * SLOTS)
    up[pl.ds(7 * N, TILE), :] = tile
    down[pl.ds(7 * N, TILE), :] = tile
    for ref, x in ((far, parity[0]), (near, 1 - parity[0])):
        ref[pl.ds(0, TILE), :] = code_tile(retained, SLOTS * x, SLOTS)
        for i, code in enumerate((4, 1, 7)):
            place(find(x, code), ((ref, TILE + i * N),))


def step1_kernel(
    pattern, retained, parity, table, density, below, above, far, near, rel_below, rel_above,
    rows_out, far_out, near_out, buf, out, lookup, ghigh, glow, sems, out_sems,
):
    par = parity[0]
    moves = [
        (density, 0, OWN, 8), (below, 0, BELOW, 7), (above, 0, ABOVE, 7),
        (far, TILE, LEFT + 3 * par, 3), (near, TILE, RIGHT - 3 * par, 3),
        (rel_below, TILE, CORNER + par, 1), (rel_below, 2 * TILE + N, CORNER + 1 - par, 1),
        (rel_above, TILE, CORNER + 2 + par, 1), (rel_above, 2 * TILE + N, CORNER + 3 - par, 1),
    ]
    copies = []
    for i, (src, first, block, count) in enumerate(moves):
        copy = pltpu.make_async_copy(src.at[pl.ds(first, count * N), :], buf.at[rows_of(block, count), :], sems.at[i])
        copy.start()
        copies.append(copy)

    def fill(i, _):
        lookup[i] = table[i]
        return 0

    lax.fori_loop(0, 108, fill, 0)
    for x in range(2):
        for t in range(SLOTS):
            code = pattern[SLOTS * x + t]
            a, b = offset(code)
            there = 5 + x + 4 * a + b
            block = SLOTS * x + t
            lookup[there * 9 + 8 - code] = block if t == 0 else T0 + block
    for x in range(2):
        for t in range(SLOTS):
            lookup[(5 + x) * 9 + pattern[SLOTS * x + t]] = SLOTS * x + t
    buf[rows_of(ZERO), :] = jnp.zeros((N, N), jnp.float32)
    for copy in copies:
        copy.wait()
    for block in TURNED:
        buf[rows_of(T0 + block), :] = buf[rows_of(block), :].T

    def gather(x, lefts):
        for s in range(SLOTS):
            left = lefts[SLOTS * x + s]
            a, b = offset(left)
            y = 5 + x + 4 * a + b
            for u in range(SLOTS):
                code, there = relative(left, retained[SLOTS * x + u])
                where = jnp.where(there, lookup[jnp.where(there, y * 9 + code, 0)], ZERO)
                put_factor(buf, where, ghigh, glow, s, u)

    for x in range(2):
        gather(x, pattern)
        left = jnp.concatenate([buf[rows_of(SLOTS * x + s), :] for s in range(SLOTS)], axis=1)
        square = times(left, ghigh, glow)
        gather(x, retained)
        result = 3.0 * square - 2.0 * times(square, ghigh, glow)
        pos = lax.rem(par + x, 2)
        for u in range(SLOTS):
            out[rows_of(SLOTS * pos + u), :] = result[:, u * N : (u + 1) * N]
    ends = []
    for i, (src, ref) in enumerate(((out, rows_out), (out.at[pl.ds(0, 4 * N), :], far_out), (out.at[pl.ds(4 * N, 4 * N), :], near_out))):
        copy = pltpu.make_async_copy(src, ref, out_sems.at[i])
        copy.start()
        ends.append(copy)
    for copy in ends:
        copy.wait()


def step2_kernel(
    codes, parity, table, own, below, above, far, near, far_below, far_above, near_both,
    result_out, buf, out, ghigh, glow, sems, out_sem,
):
    par = parity[0]
    moves = [
        (own, 0, 8), (below, 8, 8), (above, 16, 8), (far, 24, 4), (near, 28, 4),
        (far_below, 32, 4), (far_above, 36, 4), (near_both, 40, 8),
    ]
    copies = []
    for i, (src, block, count) in enumerate(moves):
        copy = pltpu.make_async_copy(src, buf.at[rows_of(block, count), :], sems.at[i])
        copy.start()
        copies.append(copy)
    buf[rows_of(STEP2_ZERO), :] = jnp.zeros((N, N), jnp.float32)
    for copy in copies:
        copy.wait()
    for x in range(2):
        mine = 40 + SLOTS * x
        for s in range(SLOTS):
            left = codes[mine + s]
            a, b = offset(left)
            y = 5 + x + 4 * a + b
            first_code = table[(par * 12 + y) * 2]
            first_block = table[(par * 12 + y) * 2 + 1]
            for u in range(SLOTS):
                code, there = relative(left, codes[mine + u])
                where = jnp.int32(STEP2_ZERO)
                for t in range(SLOTS):
                    where = jnp.where(there & (codes[first_code + t] == code), first_block + t, where)
                put_factor(buf, where, ghigh, glow, s, u)
        pos = lax.rem(par + x, 2)
        left = jnp.concatenate([buf[rows_of(SLOTS * pos + s), :] for s in range(SLOTS)], axis=1)
        square = times(left, ghigh, glow)
        result = times(3.0 * left - 2.0 * square, ghigh, glow)
        for u in range(SLOTS):
            out[rows_of(SLOTS * x + u), :] = result[:, u * N : (u + 1) * N]
    copy = pltpu.make_async_copy(out, result_out, out_sem)
    copy.start()
    copy.wait()


SMEM = pl.BlockSpec(memory_space=pltpu.SMEM)
VMEM = pl.BlockSpec(memory_space=pltpu.VMEM)
ANY = pl.BlockSpec(memory_space=pl.ANY)
PARAMS = pltpu.CompilerParams(vmem_limit_bytes=40 * 2**20)


def rows(count):
    return jax.ShapeDtypeStruct((count, N), jnp.float32)


def send(x, target):
    count_a, count_b = lax.axis_size("row"), lax.axis_size("col")
    pairs = []
    for a in range(count_a):
        for b in range(count_b):
            to_a, to_b = target(a, b)
            pairs.append((a * count_b + b, (to_a % count_a) * count_b + to_b % count_b))
    return lax.ppermute(x, ("row", "col"), pairs)


def to_above(x):
    return send(x, lambda a, b: (a - 1, b))


def to_below(x):
    return send(x, lambda a, b: (a + 1, b))


def to_far(x):
    return send(x, lambda a, b: (a, b + 1 if b % 2 else b - 1))


def to_near(x):
    return send(x, lambda a, b: (a, b ^ 1))


def on_device(density, pattern, retained):
    shape = density.shape
    density = density.reshape(-1, N)
    pattern = pattern.reshape(-1)
    retained = retained.reshape(-1)
    parity = jnp.full((1,), lax.axis_index("col") % 2, jnp.int32)

    up, down, far, near = pl.pallas_call(
        pack_kernel,
        out_shape=(rows(VROWS), rows(VROWS), rows(HROWS), rows(HROWS)),
        in_specs=[SMEM, SMEM, SMEM, VMEM],
        out_specs=(VMEM,) * 4,
        compiler_params=PARAMS,
    )(pattern, retained, parity, density)
    far = to_far(far)
    near = to_near(near)
    below = to_above(up)
    above = to_below(down)
    relay = jnp.concatenate([far[: TILE + N], near[: TILE + N]])
    rel_below = to_above(relay)
    rel_above = to_below(relay)

    own_rows, far_rows, near_rows = pl.pallas_call(
        step1_kernel,
        out_shape=(rows(8 * N), rows(4 * N), rows(4 * N)),
        in_specs=[SMEM] * 4 + [ANY] * 7,
        out_specs=(ANY,) * 3,
        scratch_shapes=[
            pltpu.VMEM((STEP1_BLOCKS * N, N), jnp.float32),
            pltpu.VMEM((8 * N, N), jnp.float32),
            pltpu.SMEM((108,), jnp.int32),
            pltpu.VMEM((4 * N, 4 * N), jnp.bfloat16),
            pltpu.VMEM((4 * N, 4 * N), jnp.bfloat16),
            pltpu.SemaphoreType.DMA((9,)),
            pltpu.SemaphoreType.DMA((3,)),
        ],
        compiler_params=PARAMS,
    )(pattern, retained, parity, jnp.asarray(ring_table()), density, below, above, far, near, rel_below, rel_above)

    codes = jnp.concatenate(
        [
            below[7 * N, :8], above[7 * N, :8], far[0, :4], near[0, :4],
            rel_below[0, :4], rel_below[TILE + N, :4], rel_above[0, :4], rel_above[TILE + N, :4],
        ]
    ).astype(jnp.int32)
    codes = jnp.concatenate([codes, retained])

    far = to_far(far_rows)
    below = to_above(own_rows)
    above = to_below(own_rows)
    near = to_near(near_rows)
    far_below = to_above(far)
    far_above = to_below(far)
    near_both = to_near(jnp.concatenate([above[4 * N :], below[4 * N :]]))

    result = pl.pallas_call(
        step2_kernel,
        out_shape=rows(8 * N),
        in_specs=[SMEM] * 3 + [ANY] * 8,
        out_specs=ANY,
        scratch_shapes=[
            pltpu.VMEM((STEP2_BLOCKS * N, N), jnp.float32),
            pltpu.VMEM((8 * N, N), jnp.float32),
            pltpu.VMEM((4 * N, 4 * N), jnp.bfloat16),
            pltpu.VMEM((4 * N, 4 * N), jnp.bfloat16),
            pltpu.SemaphoreType.DMA((8,)),
            pltpu.SemaphoreType.DMA,
        ],
        compiler_params=PARAMS,
    )(codes, parity, jnp.asarray(FAR_TABLE.reshape(-1)), own_rows, below, above, far, near, far_below, far_above, near_both)
    return result.reshape(shape)


def solution(mesh):
    return jax.shard_map(
        on_device,
        mesh=mesh,
        in_specs=(P("row", "col", None, None, None), P("row", "col", None), P("row", "col", None)),
        out_specs=P("row", "col", None, None, None),
        check_vma=False,
    )
```

```python
import jax
import jax.numpy as jnp
import numpy as np
from jax import lax
from jax.experimental import pallas as pl
from jax.experimental.pallas import tpu as pltpu
from jax.sharding import PartitionSpec as P

N = 128
SLOTS = 4
GROUP = 4
TILE = 8
H = N // 2
SELF = TILE + H
VROWS = TILE + 2 * H + 5 * N
HROWS = SELF + 2 * N
NROWS = HROWS + 2 * SELF


OWN, BELOW, ABOVE, LEFT, RIGHT, CORNER, ZERO, T0 = 0, 8, 15, 22, 25, 28, 32, 33
STEP1_BLOCKS = 65


def ring_table():
    m = np.full((12, 9), ZERO, np.int32)
    for p, b in ((9, 28), (9, 8), (8, 28), (11, 29), (0, 30), (3, 31)):
        m[p, 4] = b
    m[9, 4], m[10, 4], m[1, 4], m[2, 4] = BELOW, BELOW + 1, ABOVE, ABOVE + 1
    m[4, 4], m[7, 4] = LEFT, RIGHT

    def edge(p, code, block):
        m[p, code] = block
        m[p + (code // 3 - 1) * 4 + code % 3 - 1, 8 - code] = T0 + block

    for base, p, left, right in ((BELOW, 9, 0, 2), (ABOVE, 1, 6, 8)):
        edge(p, 5, base + 2)
        edge(p, 3, base + 3)
        edge(p + 1, 5, base + 4)
        edge(p, left, base + 5)
        edge(p + 1, right, base + 6)
    for base, p in ((LEFT, 4), (RIGHT, 7)):
        edge(p, 1, base + 1)
        edge(p, 7, base + 2)
    return m.reshape(-1)


TURNED = [s for s in range(1, 4)] + [4 + s for s in range(1, 4)]
TURNED += [b + i for b in (BELOW, ABOVE) for i in range(2, 7)]
TURNED += [b + i for b in (LEFT, RIGHT) for i in (1, 2)]

FAR_TABLE = np.zeros((2, 12, 3), np.int32)
for parity in range(2):
    far, near = (0, 3) if parity == 0 else (3, 0)
    for x in range(2):
        pos = x ^ parity
        FAR_TABLE[parity, 5 + x] = 8, 4 * x, 4 * pos
        FAR_TABLE[parity, 9 + x] = 0, 4 - 4 * pos, 8 + 4 * pos
        FAR_TABLE[parity, 1 + x] = 1, 4 - 4 * pos, 16 + 4 * pos
    FAR_TABLE[parity, 4 + far] = 2, 0, 24
    FAR_TABLE[parity, 4 + near] = 3, 0, 48
    FAR_TABLE[parity, 8 + far] = 4, 0, 32
    FAR_TABLE[parity, 8 + near] = 6, 0, 44
    FAR_TABLE[parity, 0 + far] = 5, 0, 36
    FAR_TABLE[parity, 0 + near] = 7, 0, 40
STEP2_ZERO = 28
STEP2_BLOCKS = 52


def rows_of(block, count=1):
    if isinstance(block, int):
        return pl.ds(block * N, count * N)
    return pl.ds(pl.multiple_of(block * N, N), count * N)


def offset(code):
    return lax.div(code, 3) - 1, lax.rem(code, 3) - 1


def relative(left, out):
    la, lb = offset(left)
    oa, ob = offset(out)
    a, b = oa - la, ob - lb
    near = (a >= -1) & (a <= 1) & (b >= -1) & (b <= 1)
    return (a + 1) * 3 + b + 1, near


def halves(value):
    high = value.astype(jnp.bfloat16)
    return high, (value - high.astype(jnp.float32)).astype(jnp.bfloat16)


def put_factor(buf, where, high_ref, low_ref, s, u):
    high, low = halves(buf[rows_of(where), :])
    at = (pl.ds(s * N, N), pl.ds(u * N, N))
    high_ref[at] = high
    low_ref[at] = low


def times(left, high_ref, low_ref):
    high, low = halves(left)
    both = jnp.dot(jnp.concatenate([high, low], axis=0), high_ref[...], preferred_element_type=jnp.float32)
    return both[:N] + both[N:] + jnp.dot(high, low_ref[...], preferred_element_type=jnp.float32)


def code_tile(codes, x):
    lane = lax.broadcasted_iota(jnp.int32, (TILE, N), 1)
    tile = jnp.zeros((TILE, N), jnp.float32)
    for j in range(SLOTS):
        tile = jnp.where(lane == j, codes[0, x, j].astype(jnp.float32), tile)
    return tile


def packed(block):
    row, lane = (lax.broadcasted_iota(jnp.int32, (H, N), d) for d in range(2))
    top, bottom = block[:H], block[H:]
    diagonal = jnp.sum(jnp.where(lane == row + H, bottom, 0.0), axis=0, keepdims=True)
    return jnp.where((lane < H) & (row > lane), pltpu.roll(bottom, H, 1), top), diagonal


def unpacked(half, diagonal):
    row, lane = (lax.broadcasted_iota(jnp.int32, (H, N), d) for d in range(2))
    turned = jnp.concatenate([half, jnp.zeros((H, N), jnp.float32)], axis=0).T
    top = jnp.where((lane < H) & (row > lane), turned[:H], half)
    upper = jnp.where(row == lane - H, jnp.broadcast_to(diagonal, (H, N)), pltpu.roll(turned[:H], H, 1))
    return top, jnp.where(lane < H, turned[H:], jnp.where(row > lane - H, pltpu.roll(half, H, 1), upper))


def pack_kernel(pattern, retained, parity, density, up, down, far, near):
    def find(x, code):
        slot = jnp.int32(-1)
        for t in range(SLOTS):
            slot = jnp.where(pattern[0, x, t] == code, SLOTS * x + t, slot)
        return slot

    def place(slot, targets):
        block = density[rows_of(jnp.maximum(slot, 0)), :] * (slot >= 0).astype(jnp.float32)
        for ref, first in targets:
            ref[pl.ds(first, N), :] = block

    par = parity[0]
    edges = TILE + 2 * H
    for i, (x, code) in enumerate(((0, 5), (0, 3), (1, 5))):
        place(find(x, code), ((up, edges + i * N), (down, edges + i * N)))
    place(find(0, 0), ((up, edges + 3 * N),))
    place(find(1, 2), ((up, edges + 4 * N),))
    place(find(0, 6), ((down, edges + 3 * N),))
    place(find(1, 8), ((down, edges + 4 * N),))
    far_half, far_diagonal = packed(density[rows_of(SLOTS * par), :])
    near_half, near_diagonal = packed(density[rows_of(SLOTS * (1 - par)), :])
    far_tile = code_tile(retained, par)
    near_tile = code_tile(retained, 1 - par)
    row = lax.broadcasted_iota(jnp.int32, (TILE, N), 0)
    tile = jnp.where(row == 0, near_tile + pltpu.roll(far_tile, SLOTS, 1), 0.0)
    tile = jnp.where(row == 1, near_diagonal, jnp.where(row == 2, far_diagonal, tile))
    for ref in (up, down):
        ref[pl.ds(0, TILE), :] = tile
        ref[pl.ds(TILE, H), :] = near_half
        ref[pl.ds(TILE + H, H), :] = far_half
    sides = ((far, par, far_tile, far_diagonal, far_half), (near, 1 - par, near_tile, near_diagonal, near_half))
    for ref, x, tile, diagonal, half in sides:
        ref[pl.ds(0, TILE), :] = jnp.where(row == 1, diagonal, tile)
        ref[pl.ds(TILE, H), :] = half
        for i, code in enumerate((1, 7)):
            place(find(x, code), ((ref, SELF + i * N),))


def step1_kernel(
    pattern, retained, parity, table, density, below, above, far, rel_below, rel_above, near_all,
    rows_out, far_out, codes_out, buf, heads, codes, out, lookup, ghigh, glow, sems, out_sems,
):
    par = parity[0]
    edges = TILE + 2 * H
    moves = [
        (density, 0, OWN, 8), (below, edges, BELOW + 2, 5), (above, edges, ABOVE + 2, 5),
        (far, SELF, LEFT + 1 + 3 * par, 2), (near_all, SELF, RIGHT + 1 - 3 * par, 2),
    ]
    parts = [
        (below, 0, edges, ((BELOW + 1 - par, TILE, 1), (BELOW + par, SELF, 2))),
        (above, 0, edges, ((ABOVE + 1 - par, TILE, 1), (ABOVE + par, SELF, 2))),
        (far, 0, SELF, ((LEFT + 3 * par, TILE, 1),)),
        (near_all, 0, SELF, ((RIGHT - 3 * par, TILE, 1),)),
        (rel_below, 0, SELF, ((CORNER + par, TILE, 1),)),
        (rel_above, 0, SELF, ((CORNER + 2 + par, TILE, 1),)),
        (near_all, HROWS, SELF, ((CORNER + 1 - par, TILE, 1),)),
        (near_all, HROWS + SELF, SELF, ((CORNER + 3 - par, TILE, 1),)),
    ]
    copies = []
    for i, (src, first, block, count) in enumerate(moves):
        copy = pltpu.make_async_copy(src.at[pl.ds(first, count * N), :], buf.at[rows_of(block, count), :], sems.at[i])
        copy.start()
        copies.append(copy)
    at, halves_at, tiles_at = 0, [], []
    for i, (src, first, count, selves) in enumerate(parts):
        copy = pltpu.make_async_copy(src.at[pl.ds(first, count), :], heads.at[pl.ds(at, count), :], sems.at[len(moves) + i])
        copy.start()
        copies.append(copy)
        halves_at += [(block, at + half, at + diagonal) for block, half, diagonal in selves]
        tiles_at.append(at)
        at += count

    def fill(i, _):
        lookup[i] = table[i]
        return 0

    lax.fori_loop(0, 108, fill, 0)
    for x in range(2):
        for t in range(SLOTS):
            code = pattern[0, x, t]
            a, b = offset(code)
            there = 5 + x + 4 * a + b
            block = SLOTS * x + t
            lookup[there * 9 + 8 - code] = block if t == 0 else T0 + block
    for x in range(2):
        for t in range(SLOTS):
            lookup[(5 + x) * 9 + pattern[0, x, t]] = SLOTS * x + t
    buf[rows_of(ZERO), :] = jnp.zeros((N, N), jnp.float32)
    for copy in copies:
        copy.wait()
    row = lax.broadcasted_iota(jnp.int32, (TILE, N), 0)
    tile = jnp.zeros((TILE, N), jnp.float32)
    for i, at in enumerate(tiles_at):
        tile = jnp.where(row == i, jnp.broadcast_to(heads[pl.ds(at, 1), :], (TILE, N)), tile)
    codes[...] = tile
    for block, half, diagonal in halves_at:
        top, bottom = unpacked(heads[pl.ds(half, H), :], heads[pl.ds(diagonal, 1), :])
        buf[rows_of(block), :] = jnp.concatenate([top, bottom], axis=0)
    for block in TURNED:
        buf[rows_of(T0 + block), :] = buf[rows_of(block), :].T

    def gather(x, lefts):
        for s in range(SLOTS):
            left = lefts[0, x, s]
            a, b = offset(left)
            y = 5 + x + 4 * a + b
            for u in range(SLOTS):
                code, there = relative(left, retained[0, x, u])
                where = jnp.where(there, lookup[jnp.where(there, y * 9 + code, 0)], ZERO)
                put_factor(buf, where, ghigh, glow, s, u)

    for x in range(2):
        gather(x, pattern)
        left = jnp.concatenate([buf[rows_of(SLOTS * x + s), :] for s in range(SLOTS)], axis=1)
        square = times(left, ghigh, glow)
        gather(x, retained)
        result = 3.0 * square - 2.0 * times(square, ghigh, glow)
        pos = lax.rem(par + x, 2)
        for u in range(SLOTS):
            out[rows_of(SLOTS * pos + u), :] = result[:, u * N : (u + 1) * N]
    ends = []
    for i, (src, ref) in enumerate(((out.at[pl.ds(0, 4 * N), :], far_out), (out, rows_out), (codes, codes_out))):
        copy = pltpu.make_async_copy(src, ref, out_sems.at[i])
        copy.start()
        ends.append(copy)
    for copy in ends:
        copy.wait()


def step2_kernel(
    retained, parity, table, codes_in, own, below, above, far, far_below, far_above, near_all,
    result_out, codes, buf, out, ghigh, glow, sems, out_sem,
):
    par = parity[0]
    moves = [
        (own, 0, 8), (below, 8, 8), (above, 16, 8), (far, 24, 4),
        (far_below, 32, 4), (far_above, 36, 4), (near_all, 40, 12),
    ]
    copies = []
    for i, (src, block, count) in enumerate(moves):
        copy = pltpu.make_async_copy(src, buf.at[rows_of(block, count), :], sems.at[i])
        copy.start()
        copies.append(copy)
    copy = pltpu.make_async_copy(codes_in, codes.at[pl.ds(0, TILE), :], sems.at[len(moves)])
    copy.start()
    copies.append(copy)
    for t in range(2 * SLOTS):
        codes[TILE, t] = retained[0, t // SLOTS, t % SLOTS].astype(jnp.float32)
    buf[rows_of(STEP2_ZERO), :] = jnp.zeros((N, N), jnp.float32)
    for copy in copies:
        copy.wait()
    for x in range(2):
        for s in range(SLOTS):
            left = retained[0, x, s]
            a, b = offset(left)
            y = 5 + x + 4 * a + b
            entry = (par * 12 + y) * 3
            theirs = [codes[table[entry], table[entry + 1] + t].astype(jnp.int32) for t in range(SLOTS)]
            first_block = table[entry + 2]
            for u in range(SLOTS):
                code, there = relative(left, retained[0, x, u])
                where = jnp.int32(STEP2_ZERO)
                for t in range(SLOTS):
                    where = jnp.where(there & (theirs[t] == code), first_block + t, where)
                put_factor(buf, where, ghigh, glow, s, u)
        pos = lax.rem(par + x, 2)
        left = jnp.concatenate([buf[rows_of(SLOTS * pos + s), :] for s in range(SLOTS)], axis=1)
        square = times(left, ghigh, glow)
        result = times(3.0 * left - 2.0 * square, ghigh, glow)
        for u in range(SLOTS):
            out[rows_of(SLOTS * x + u), :] = result[:, u * N : (u + 1) * N]
    copy = pltpu.make_async_copy(out, result_out, out_sem)
    copy.start()
    copy.wait()


SMEM = pl.BlockSpec(memory_space=pltpu.SMEM)
VMEM = pl.BlockSpec(memory_space=pltpu.VMEM)
ANY = pl.BlockSpec(memory_space=pl.ANY)
HBM = pl.BlockSpec(memory_space=pltpu.HBM)
PARAMS = pltpu.CompilerParams(vmem_limit_bytes=40 * 2**20)


def rows(count):
    return jax.ShapeDtypeStruct((count, N), jnp.float32)


def send(x, target):
    count_a, count_b = lax.axis_size("row"), lax.axis_size("col")
    pairs = []
    for a in range(count_a):
        for b in range(count_b):
            to_a, to_b = target(a, b)
            pairs.append((a * count_b + b, (to_a % count_a) * count_b + to_b % count_b))
    return lax.ppermute(x, ("row", "col"), pairs)


def to_above(x):
    return send(x, lambda a, b: (a - 1, b))


def to_below(x):
    return send(x, lambda a, b: (a + 1, b))


def far_side(b):
    return b + 1 if b % 2 else b - 1


def corner_to_above(x):
    return send(x, lambda a, b: (a - 1, b if a % GROUP else far_side(b)))


def corner_to_below(x):
    return send(x, lambda a, b: (a + 1, b if (a + 1) % GROUP else far_side(b)))


def to_far(x):
    return send(x, lambda a, b: (a, far_side(b)))


def to_near(x):
    return send(x, lambda a, b: (a, b ^ 1))


def later_kernel(*refs):
    count = len(refs) // 2
    for given, kept in zip(refs[:count], refs[count:]):
        kept[...] = given[...]


def later(*arrays):
    count = len(arrays)
    return pl.pallas_call(
        later_kernel,
        out_shape=tuple(jax.ShapeDtypeStruct(x.shape, x.dtype) for x in arrays),
        in_specs=[VMEM] * count,
        out_specs=(VMEM,) * count,
        compiler_params=PARAMS,
    )(*arrays)


def on_device(density, pattern, retained):
    shape = density.shape
    density = density.reshape(-1, N)
    parity = jnp.full((1,), lax.axis_index("col") % 2, jnp.int32)

    up, down, far_sent, near = pl.pallas_call(
        pack_kernel,
        out_shape=(rows(VROWS), rows(VROWS), rows(HROWS), rows(HROWS)),
        in_specs=[SMEM, SMEM, SMEM, VMEM],
        out_specs=(VMEM,) * 4,
        compiler_params=PARAMS,
    )(pattern, retained, parity, density)
    far = to_far(far_sent)
    below = to_above(up)
    above = to_below(down)
    row = lax.axis_index("row")
    first, last = row % GROUP == 0, row % GROUP == GROUP - 1
    rel_below = corner_to_above(jnp.where(first, far_sent[:SELF], far[:SELF]))
    rel_above = corner_to_below(jnp.where(last, far_sent[:SELF], far[:SELF]))
    rel_below, rel_above = later(rel_below, rel_above)
    below, above, rel_below, rel_above = lax.optimization_barrier((below, above, rel_below, rel_above))
    near_all = to_near(jnp.concatenate([near, below[:SELF], above[:SELF]]))

    own_rows, far_rows, codes = pl.pallas_call(
        step1_kernel,
        out_shape=(rows(8 * N), rows(4 * N), rows(TILE)),
        in_specs=[SMEM] * 4 + [ANY] * 7,
        out_specs=(HBM,) * 3,
        scratch_shapes=[
            pltpu.VMEM((STEP1_BLOCKS * N, N), jnp.float32),
            pltpu.VMEM((2 * (TILE + 2 * H) + 6 * SELF, N), jnp.float32),
            pltpu.VMEM((TILE, N), jnp.float32),
            pltpu.VMEM((8 * N, N), jnp.float32),
            pltpu.SMEM((108,), jnp.int32),
            pltpu.VMEM((4 * N, 4 * N), jnp.bfloat16),
            pltpu.VMEM((4 * N, 4 * N), jnp.bfloat16),
            pltpu.SemaphoreType.DMA((13,)),
            pltpu.SemaphoreType.DMA((3,)),
        ],
        compiler_params=PARAMS,
    )(pattern, retained, parity, jnp.asarray(ring_table()), density, below, above, far, rel_below, rel_above, near_all)

    far = to_far(far_rows)
    below = to_above(own_rows)
    above = to_below(own_rows)
    far_below = corner_to_above(jnp.where(first, far_rows, far))
    far_above = corner_to_below(jnp.where(last, far_rows, far))
    far_below, far_above = later(far_below, far_above)
    above, below, far_below, far_above = lax.optimization_barrier((above, below, far_below, far_above))
    near_all = to_near(jnp.concatenate([above[4 * N :], below[4 * N :], own_rows[4 * N :]]))

    result = pl.pallas_call(
        step2_kernel,
        out_shape=rows(8 * N),
        in_specs=[SMEM] * 3 + [ANY] * 8,
        out_specs=ANY,
        scratch_shapes=[
            pltpu.SMEM((TILE + 1, N), jnp.float32),
            pltpu.VMEM((STEP2_BLOCKS * N, N), jnp.float32),
            pltpu.VMEM((8 * N, N), jnp.float32),
            pltpu.VMEM((4 * N, 4 * N), jnp.bfloat16),
            pltpu.VMEM((4 * N, 4 * N), jnp.bfloat16),
            pltpu.SemaphoreType.DMA((8,)),
            pltpu.SemaphoreType.DMA,
        ],
        compiler_params=PARAMS,
    )(retained, parity, jnp.asarray(FAR_TABLE.reshape(-1)), codes, own_rows, below, above, far, far_below, far_above, near_all)
    return result.reshape(shape)


def solution(mesh):
    return jax.shard_map(
        on_device,
        mesh=mesh,
        in_specs=(P("row", "col", None, None, None), P("row", "col", None), P("row", "col", None)),
        out_specs=P("row", "col", None, None, None),
        check_vma=False,
    )
```

```python
import functools

import jax
import jax.numpy as jnp
import numpy as np
from jax import lax
from jax.experimental import pallas as pl
from jax.experimental.pallas import tpu as pltpu
from jax.sharding import PartitionSpec as P

N = 128
SLOTS = 4
GROUP = 4
TILE = 8
H = N // 2
SELF = TILE + H
VROWS = TILE + 2 * H + 5 * N
HROWS = SELF + 2 * N
FROWS = SELF + N
NROWS = HROWS + 2 * SELF


OWN, BELOW, ABOVE, LEFT, RIGHT, CORNER, ZERO, T0 = 0, 8, 15, 22, 25, 28, 32, 33
STEP1_BLOCKS = 65


def ring_table():
    m = np.full((12, 9), ZERO, np.int32)
    for p, b in ((9, 28), (9, 8), (8, 28), (11, 29), (0, 30), (3, 31)):
        m[p, 4] = b
    m[9, 4], m[10, 4], m[1, 4], m[2, 4] = BELOW, BELOW + 1, ABOVE, ABOVE + 1
    m[4, 4], m[7, 4] = LEFT, RIGHT

    def edge(p, code, block):
        m[p, code] = block
        m[p + (code // 3 - 1) * 4 + code % 3 - 1, 8 - code] = T0 + block

    for base, p, left, right in ((BELOW, 9, 0, 2), (ABOVE, 1, 6, 8)):
        edge(p, 5, base + 2)
        edge(p, 3, base + 3)
        edge(p + 1, 5, base + 4)
        edge(p, left, base + 5)
        edge(p + 1, right, base + 6)
    for base, p in ((LEFT, 4), (RIGHT, 7)):
        edge(p, 1, base + 1)
        edge(p, 7, base + 2)
    return m.reshape(-1)


TURNED = [s for s in range(1, 4)] + [4 + s for s in range(1, 4)]
TURNED += [b + i for b in (BELOW, ABOVE) for i in range(2, 7)]

FAR_TABLE = np.zeros((2, 12, 3), np.int32)
for parity in range(2):
    far, near = (0, 3) if parity == 0 else (3, 0)
    for x in range(2):
        pos = x ^ parity
        FAR_TABLE[parity, 5 + x] = 8, 4 * x, 4 * pos
        FAR_TABLE[parity, 9 + x] = 0, 4 - 4 * pos, 8 + 4 * pos
        FAR_TABLE[parity, 1 + x] = 1, 4 - 4 * pos, 16 + 4 * pos
    FAR_TABLE[parity, 4 + far] = 2, 0, 24
    FAR_TABLE[parity, 4 + near] = 3, 0, 48
    FAR_TABLE[parity, 8 + far] = 4, 0, 32
    FAR_TABLE[parity, 8 + near] = 6, 0, 44
    FAR_TABLE[parity, 0 + far] = 5, 0, 36
    FAR_TABLE[parity, 0 + near] = 7, 0, 40
STEP2_ZERO = 28
STEP2_BLOCKS = 52


def rows_of(block, count=1):
    if isinstance(block, int):
        return pl.ds(block * N, count * N)
    return pl.ds(pl.multiple_of(block * N, N), count * N)


def offset(code):
    return lax.div(code, 3) - 1, lax.rem(code, 3) - 1


def relative(left, out):
    la, lb = offset(left)
    oa, ob = offset(out)
    a, b = oa - la, ob - lb
    near = (a >= -1) & (a <= 1) & (b >= -1) & (b <= 1)
    return (a + 1) * 3 + b + 1, near


def halves(value):
    high = value.astype(jnp.bfloat16)
    return high, (value - high.astype(jnp.float32)).astype(jnp.bfloat16)


def put_factor(buf, where, high_ref, low_ref, s, u):
    high, low = halves(buf[rows_of(where), :])
    at = (pl.ds(s * N, N), pl.ds(u * N, N))
    high_ref[at] = high
    low_ref[at] = low


def times(left, high_ref, low_ref):
    high, low = halves(left)
    both = jnp.dot(jnp.concatenate([high, low], axis=0), high_ref[...], preferred_element_type=jnp.float32)
    return both[:N] + both[N:] + jnp.dot(high, low_ref[...], preferred_element_type=jnp.float32)


def code_tile(codes, x):
    lane = lax.broadcasted_iota(jnp.int32, (TILE, N), 1)
    tile = jnp.zeros((TILE, N), jnp.float32)
    for j in range(SLOTS):
        tile = jnp.where(lane == j, codes[0, x, j].astype(jnp.float32), tile)
    return tile


def packed(block):
    row, lane = (lax.broadcasted_iota(jnp.int32, (H, N), d) for d in range(2))
    top, bottom = block[:H], block[H:]
    diagonal = jnp.sum(jnp.where(lane == row + H, bottom, 0.0), axis=0, keepdims=True)
    return jnp.where((lane < H) & (row > lane), pltpu.roll(bottom, H, 1), top), diagonal


def unpacked(half, diagonal):
    row, lane = (lax.broadcasted_iota(jnp.int32, (H, N), d) for d in range(2))
    turned = jnp.concatenate([half, jnp.zeros((H, N), jnp.float32)], axis=0).T
    top = jnp.where((lane < H) & (row > lane), turned[:H], half)
    upper = jnp.where(row == lane - H, jnp.broadcast_to(diagonal, (H, N)), pltpu.roll(turned[:H], H, 1))
    return top, jnp.where(lane < H, turned[H:], jnp.where(row > lane - H, pltpu.roll(half, H, 1), upper))


def pack_kernel(pattern, retained, parity, density, up, down, far, near):
    def find(x, code):
        slot = jnp.int32(-1)
        for t in range(SLOTS):
            slot = jnp.where(pattern[0, x, t] == code, SLOTS * x + t, slot)
        return slot

    def place(slot, targets):
        block = density[rows_of(jnp.maximum(slot, 0)), :] * (slot >= 0).astype(jnp.float32)
        for ref, first in targets:
            ref[pl.ds(first, N), :] = block

    par = parity[0]
    edges = TILE + 2 * H
    for i, (x, code) in enumerate(((0, 5), (0, 3), (1, 5))):
        place(find(x, code), ((up, edges + i * N), (down, edges + i * N)))
    place(find(0, 0), ((up, edges + 3 * N),))
    place(find(1, 2), ((up, edges + 4 * N),))
    place(find(0, 6), ((down, edges + 3 * N),))
    place(find(1, 8), ((down, edges + 4 * N),))
    far_half, far_diagonal = packed(density[rows_of(SLOTS * par), :])
    near_half, near_diagonal = packed(density[rows_of(SLOTS * (1 - par)), :])
    far_tile = code_tile(retained, par)
    near_tile = code_tile(retained, 1 - par)
    row = lax.broadcasted_iota(jnp.int32, (TILE, N), 0)
    tile = jnp.where(row == 0, near_tile + pltpu.roll(far_tile, SLOTS, 1), 0.0)
    tile = jnp.where(row == 1, near_diagonal, jnp.where(row == 2, far_diagonal, tile))
    for ref in (up, down):
        ref[pl.ds(0, TILE), :] = tile
        ref[pl.ds(TILE, H), :] = near_half
        ref[pl.ds(TILE + H, H), :] = far_half
    sides = ((far, par, far_tile, far_diagonal, far_half, (7,)), (near, 1 - par, near_tile, near_diagonal, near_half, (1, 7)))
    for ref, x, tile, diagonal, half, codes in sides:
        ref[pl.ds(0, TILE), :] = jnp.where(row == 1, diagonal, tile)
        ref[pl.ds(TILE, H), :] = half
        for i, code in enumerate(codes):
            place(find(x, code), ((ref, SELF + i * N),))


def step1_kernel(
    pattern, retained, parity, table, density, below, above, far, rel_below, rel_above, near_all,
    rows_out, far_out, codes_out, buf, heads, codes, out, lookup, ghigh, glow, sems, out_sems, table_sem,
):
    par = parity[0]
    table_copy = pltpu.make_async_copy(table, lookup, table_sem)
    table_copy.start()
    edges = TILE + 2 * H
    moves = [
        (density, 0, OWN, 8), (below, edges, BELOW + 2, 5), (above, edges, ABOVE + 2, 5),
        (far, SELF, LEFT + 2 + 3 * par, 1), (near_all, SELF, RIGHT + 1 - 3 * par, 2),
        (rel_above, SELF, T0 + LEFT + 1 + 3 * par, 1),
    ]
    parts = [
        (below, 0, edges, ((BELOW + 1 - par, TILE, 1), (BELOW + par, SELF, 2))),
        (above, 0, edges, ((ABOVE + 1 - par, TILE, 1), (ABOVE + par, SELF, 2))),
        (far, 0, SELF, ((LEFT + 3 * par, TILE, 1),)),
        (near_all, 0, SELF, ((RIGHT - 3 * par, TILE, 1),)),
        (rel_below, 0, SELF, ((CORNER + par, TILE, 1),)),
        (rel_above, 0, SELF, ((CORNER + 2 + par, TILE, 1),)),
        (near_all, HROWS, SELF, ((CORNER + 1 - par, TILE, 1),)),
        (near_all, HROWS + SELF, SELF, ((CORNER + 3 - par, TILE, 1),)),
    ]
    copies = []
    for i, (src, first, block, count) in enumerate(moves):
        copy = pltpu.make_async_copy(src.at[pl.ds(first, count * N), :], buf.at[rows_of(block, count), :], sems.at[i])
        copy.start()
        copies.append(copy)
    at, halves_at, tiles_at = 0, [], []
    for i, (src, first, count, selves) in enumerate(parts):
        copy = pltpu.make_async_copy(src.at[pl.ds(first, count), :], heads.at[pl.ds(at, count), :], sems.at[len(moves) + i])
        copy.start()
        copies.append(copy)
        halves_at += [(block, at + half, at + diagonal) for block, half, diagonal in selves]
        tiles_at.append(at)
        at += count

    table_copy.wait()
    for x in range(2):
        for t in range(SLOTS):
            code = pattern[0, x, t]
            a, b = offset(code)
            there = 5 + x + 4 * a + b
            block = SLOTS * x + t
            lookup[there * 9 + 8 - code] = block if t == 0 else T0 + block
    for x in range(2):
        for t in range(SLOTS):
            lookup[(5 + x) * 9 + pattern[0, x, t]] = SLOTS * x + t
    buf[rows_of(ZERO), :] = jnp.zeros((N, N), jnp.float32)
    for copy in copies:
        copy.wait()
    row = lax.broadcasted_iota(jnp.int32, (TILE, N), 0)
    tile = jnp.zeros((TILE, N), jnp.float32)
    for i, at in enumerate(tiles_at):
        tile = jnp.where(row == i, jnp.broadcast_to(heads[pl.ds(at, 1), :], (TILE, N)), tile)
    codes[...] = tile
    for block, half, diagonal in halves_at:
        top, bottom = unpacked(heads[pl.ds(half, H), :], heads[pl.ds(diagonal, 1), :])
        buf[rows_of(block), :] = jnp.concatenate([top, bottom], axis=0)
    far_up, near_up = LEFT + 1 + 3 * par, RIGHT + 1 - 3 * par
    turned = [(block, T0 + block) for block in (*TURNED, far_up + 1, near_up, near_up + 1)] + [(T0 + far_up, far_up)]
    for block, other in turned:
        buf[rows_of(other), :] = buf[rows_of(block), :].T

    def gather(x, lefts):
        for s in range(SLOTS):
            left = lefts[0, x, s]
            a, b = offset(left)
            y = 5 + x + 4 * a + b
            for u in range(SLOTS):
                code, there = relative(left, retained[0, x, u])
                where = jnp.where(there, lookup[jnp.where(there, y * 9 + code, 0)], ZERO)
                put_factor(buf, where, ghigh, glow, s, u)

    for x in range(2):
        gather(x, pattern)
        left = jnp.concatenate([buf[rows_of(SLOTS * x + s), :] for s in range(SLOTS)], axis=1)
        square = times(left, ghigh, glow)
        gather(x, retained)
        result = 3.0 * square - 2.0 * times(square, ghigh, glow)
        pos = lax.rem(par + x, 2)
        for u in range(SLOTS):
            out[rows_of(SLOTS * pos + u), :] = result[:, u * N : (u + 1) * N]
    ends = []
    for i, (src, ref) in enumerate(((out.at[pl.ds(0, 4 * N), :], far_out), (out, rows_out), (codes, codes_out))):
        copy = pltpu.make_async_copy(src, ref, out_sems.at[i])
        copy.start()
        ends.append(copy)
    for copy in ends:
        copy.wait()


def start(copies, src, dst, sems):
    copy = pltpu.make_async_copy(src, dst, sems.at[len(copies)])
    copy.start()
    copies.append(copy)


def finish(copies):
    for copy in copies:
        copy.wait()


def step2_kernel(side, retained, parity, table, codes_in, own, below, above, *refs):
    par = parity[0]
    moves = [(own, 0, 8), (below, 8, 8), (above, 16, 8)]
    if side == "far":
        x = par
        moves += [(refs[0], 24, 4), (refs[1], 32, 4), (refs[2], 36, 4)]
        result_out = refs[3]
    else:
        x = 1 - par
        moves += [(refs[0], 40, 12)]
        far_result, result_out = refs[1:3]
    codes, buf, out, ghigh, glow, sems, out_sems = refs[-7:]
    copies, written = [], []
    start(copies, codes_in, codes.at[pl.ds(0, TILE), :], sems)
    for src, block, count in moves:
        start(copies, src, buf.at[rows_of(block, count), :], sems)
    if side == "near":
        start(written, far_result, result_out.at[rows_of(SLOTS * par, SLOTS), :], out_sems)
    for t in range(2 * SLOTS):
        codes[TILE, t] = retained[0, t // SLOTS, t % SLOTS].astype(jnp.float32)
    buf[rows_of(STEP2_ZERO), :] = jnp.zeros((N, N), jnp.float32)
    copies[0].wait()
    places = []
    for s in range(SLOTS):
        left = retained[0, x, s]
        a, b = offset(left)
        entry = (par * 12 + 5 + x + 4 * a + b) * 3
        theirs = [codes[table[entry], table[entry + 1] + t].astype(jnp.int32) for t in range(SLOTS)]
        first_block = table[entry + 2]
        for u in range(SLOTS):
            code, there = relative(left, retained[0, x, u])
            where = jnp.int32(STEP2_ZERO)
            for t in range(SLOTS):
                where = jnp.where(there & (theirs[t] == code), first_block + t, where)
            places.append((where, s, u))
    finish(copies[1:])
    for where, s, u in places:
        put_factor(buf, where, ghigh, glow, s, u)
    mine = 0 if side == "far" else SLOTS
    left = jnp.concatenate([buf[rows_of(mine + s), :] for s in range(SLOTS)], axis=1)
    square = times(left, ghigh, glow)
    result = times(3.0 * left - 2.0 * square, ghigh, glow)
    for u in range(SLOTS):
        out[rows_of(u), :] = result[:, u * N : (u + 1) * N]
    if side == "near":
        start(written, out, result_out.at[rows_of(SLOTS * x, SLOTS), :], out_sems)
    else:
        start(written, out, result_out, out_sems)
    finish(written)


SMEM = pl.BlockSpec(memory_space=pltpu.SMEM)
VMEM = pl.BlockSpec(memory_space=pltpu.VMEM)
ANY = pl.BlockSpec(memory_space=pl.ANY)
COST = pl.CostEstimate(flops=10**11, bytes_accessed=10**8, transcendentals=0)
HBM = pl.BlockSpec(memory_space=pltpu.HBM)
PARAMS = pltpu.CompilerParams(vmem_limit_bytes=40 * 2**20)


FACTOR = [pltpu.VMEM((4 * N, 4 * N), jnp.bfloat16)] * 2


def step2(side, out_rows, *args):
    return pl.pallas_call(
        functools.partial(step2_kernel, side),
        out_shape=rows(out_rows),
        in_specs=[SMEM] * 3 + [ANY] * (len(args) - 2),
        out_specs=ANY,
        scratch_shapes=[
            pltpu.SMEM((TILE + 1, N), jnp.float32),
            pltpu.VMEM((STEP2_BLOCKS * N, N), jnp.float32),
            pltpu.VMEM((4 * N, N), jnp.float32),
            *FACTOR,
            pltpu.SemaphoreType.DMA((7,)),
            pltpu.SemaphoreType.DMA((2,)),
        ],
        compiler_params=PARAMS,
    )(*args[:2], jnp.asarray(FAR_TABLE.reshape(-1)), *args[2:])


def rows(count):
    return jax.ShapeDtypeStruct((count, N), jnp.float32)


def send(x, target):
    count_a, count_b = lax.axis_size("row"), lax.axis_size("col")
    pairs = []
    for a in range(count_a):
        for b in range(count_b):
            to_a, to_b = target(a, b)
            pairs.append((a * count_b + b, (to_a % count_a) * count_b + to_b % count_b))
    return lax.ppermute(x, ("row", "col"), pairs)


def to_above(x):
    return send(x, lambda a, b: (a - 1, b))


def to_below(x):
    return send(x, lambda a, b: (a + 1, b))


def far_side(b):
    return b + 1 if b % 2 else b - 1


def corner_to_above(x):
    return send(x, lambda a, b: (a - 1, b if a % GROUP else far_side(b)))


def corner_to_below(x):
    return send(x, lambda a, b: (a + 1, b if (a + 1) % GROUP else far_side(b)))


def to_far(x):
    return send(x, lambda a, b: (a, far_side(b)))


def to_near(x):
    return send(x, lambda a, b: (a, b ^ 1))


def corner_kernel(row, mine, theirs, to_above, to_below):
    line = lax.rem(row[0], GROUP)
    for there, out in ((0, to_above), (GROUP - 1, to_below)):
        part = pl.ds(0, out.shape[0])

        @pl.when(line == there)
        def _():
            out[...] = mine[part, :]

        @pl.when(line != there)
        def _():
            out[...] = theirs[part, :]


def corners(mine, theirs, above_rows):
    to_above, to_below = pl.pallas_call(
        corner_kernel,
        out_shape=(rows(above_rows), rows(mine.shape[0])),
        in_specs=[SMEM, VMEM, VMEM],
        out_specs=(VMEM, VMEM),
        compiler_params=PARAMS,
        cost_estimate=COST,
    )(jnp.full((1,), lax.axis_index("row"), jnp.int32), mine, theirs)
    return corner_to_above(to_above), corner_to_below(to_below)


def on_device(density, pattern, retained):
    shape = density.shape
    density = density.reshape(-1, N)
    parity = jnp.full((1,), lax.axis_index("col") % 2, jnp.int32)

    up, down, far_sent, near = pl.pallas_call(
        pack_kernel,
        out_shape=(rows(VROWS), rows(VROWS), rows(FROWS), rows(HROWS)),
        in_specs=[SMEM, SMEM, SMEM, VMEM],
        out_specs=(VMEM,) * 4,
        compiler_params=PARAMS,
    )(pattern, retained, parity, density)
    far = to_far(far_sent)
    below = to_above(up)
    above = to_below(down)
    rel_below, rel_above = corners(far_sent, far, SELF)
    below, above, rel_below, rel_above = lax.optimization_barrier((below, above, rel_below, rel_above))
    near_all = to_near(jnp.concatenate([near, below[:SELF], above[:SELF]]))

    own_rows, far_rows, codes = pl.pallas_call(
        step1_kernel,
        out_shape=(rows(8 * N), rows(4 * N), rows(TILE)),
        in_specs=[SMEM] * 3 + [ANY] * 8,
        out_specs=(HBM,) * 3,
        scratch_shapes=[
            pltpu.VMEM((STEP1_BLOCKS * N, N), jnp.float32),
            pltpu.VMEM((2 * (TILE + 2 * H) + 6 * SELF, N), jnp.float32),
            pltpu.VMEM((TILE, N), jnp.float32),
            pltpu.VMEM((8 * N, N), jnp.float32),
            pltpu.SMEM((108,), jnp.int32),
            pltpu.VMEM((4 * N, 4 * N), jnp.bfloat16),
            pltpu.VMEM((4 * N, 4 * N), jnp.bfloat16),
            pltpu.SemaphoreType.DMA((14,)),
            pltpu.SemaphoreType.DMA((3,)),
            pltpu.SemaphoreType.DMA,
        ],
        compiler_params=PARAMS,
    )(pattern, retained, parity, jnp.asarray(ring_table()), density, below, above, far, rel_below, rel_above, near_all)

    far = to_far(far_rows)
    below = to_above(own_rows)
    above = to_below(own_rows)
    far_below, far_above = corners(far_rows, far, 4 * N)
    below, above, far_below, far_above = lax.optimization_barrier((below, above, far_below, far_above))
    near_all = to_near(jnp.concatenate([above[4 * N :], below[4 * N :], own_rows[4 * N :]]))
    shared = (retained, parity, codes, own_rows, below, above)
    result = step2("far", 4 * N, *shared, far, far_below, far_above)
    result = step2("near", 8 * N, *shared, near_all, result)
    return result.reshape(shape)


def solution(mesh):
    return jax.shard_map(
        on_device,
        mesh=mesh,
        in_specs=(P("row", "col", None, None, None), P("row", "col", None), P("row", "col", None)),
        out_specs=P("row", "col", None, None, None),
        check_vma=False,
    )
```

```python
import functools

import jax
import jax.numpy as jnp
import numpy as np
from jax import lax
from jax.experimental import pallas as pl
from jax.experimental.pallas import tpu as pltpu
from jax.sharding import PartitionSpec as P

N = 128
SLOTS = 4
GROUP = 4
TILE = 8
H = N // 2
SELF = TILE + H
VROWS = TILE + 2 * H + 5 * N
HROWS = SELF + 2 * N
FROWS = SELF + N
NROWS = HROWS + 2 * SELF


OWN, BELOW, ABOVE, LEFT, RIGHT, CORNER, ZERO, T0 = 0, 8, 15, 22, 25, 28, 32, 33
STEP1_BLOCKS = 65


def ring_table():
    m = np.full((12, 9), ZERO, np.int32)
    for p, b in ((9, 28), (9, 8), (8, 28), (11, 29), (0, 30), (3, 31)):
        m[p, 4] = b
    m[9, 4], m[10, 4], m[1, 4], m[2, 4] = BELOW, BELOW + 1, ABOVE, ABOVE + 1
    m[4, 4], m[7, 4] = LEFT, RIGHT

    def edge(p, code, block):
        m[p, code] = block
        m[p + (code // 3 - 1) * 4 + code % 3 - 1, 8 - code] = T0 + block

    for base, p, left, right in ((BELOW, 9, 0, 2), (ABOVE, 1, 6, 8)):
        edge(p, 5, base + 2)
        edge(p, 3, base + 3)
        edge(p + 1, 5, base + 4)
        edge(p, left, base + 5)
        edge(p + 1, right, base + 6)
    for base, p in ((LEFT, 4), (RIGHT, 7)):
        edge(p, 1, base + 1)
        edge(p, 7, base + 2)
    return m.reshape(-1)


TURNED = [s for s in range(1, 4)] + [4 + s for s in range(1, 4)]
TURNED += [b + i for b in (BELOW, ABOVE) for i in range(2, 7)]

FAR_TABLE = np.zeros((2, 12, 3), np.int32)
for parity in range(2):
    far, near = (0, 3) if parity == 0 else (3, 0)
    for x in range(2):
        pos = x ^ parity
        FAR_TABLE[parity, 5 + x] = 8, 4 * x, 4 * pos
        FAR_TABLE[parity, 9 + x] = 0, 4 - 4 * pos, 8 + 4 * pos
        FAR_TABLE[parity, 1 + x] = 1, 4 - 4 * pos, 16 + 4 * pos
    FAR_TABLE[parity, 4 + far] = 2, 0, 24
    FAR_TABLE[parity, 4 + near] = 3, 0, 48
    FAR_TABLE[parity, 8 + far] = 4, 0, 32
    FAR_TABLE[parity, 8 + near] = 6, 0, 44
    FAR_TABLE[parity, 0 + far] = 5, 0, 36
    FAR_TABLE[parity, 0 + near] = 7, 0, 40
STEP2_ZERO = 28
STEP2_BLOCKS = 52


def rows_of(block, count=1):
    if isinstance(block, int):
        return pl.ds(block * N, count * N)
    return pl.ds(pl.multiple_of(block * N, N), count * N)


def offset(code):
    return lax.div(code, 3) - 1, lax.rem(code, 3) - 1


def relative(left, out):
    la, lb = offset(left)
    oa, ob = offset(out)
    a, b = oa - la, ob - lb
    near = (a >= -1) & (a <= 1) & (b >= -1) & (b <= 1)
    return (a + 1) * 3 + b + 1, near


def halves(value):
    high = value.astype(jnp.bfloat16)
    return high, (value - high.astype(jnp.float32)).astype(jnp.bfloat16)


def put_factor(buf, where, high_ref, low_ref, s, u):
    high, low = halves(buf[rows_of(where), :])
    at = (pl.ds(s * N, N), pl.ds(u * N, N))
    high_ref[at] = high
    low_ref[at] = low


def times(left, high_ref, low_ref):
    high, low = halves(left)
    both = jnp.dot(jnp.concatenate([high, low], axis=0), high_ref[...], preferred_element_type=jnp.float32)
    return both[:N] + both[N:] + jnp.dot(high, low_ref[...], preferred_element_type=jnp.float32)


def code_tile(codes, x):
    lane = lax.broadcasted_iota(jnp.int32, (TILE, N), 1)
    tile = jnp.zeros((TILE, N), jnp.float32)
    for j in range(SLOTS):
        tile = jnp.where(lane == j, codes[0, x, j].astype(jnp.float32), tile)
    return tile


def packed(block):
    row, lane = (lax.broadcasted_iota(jnp.int32, (H, N), d) for d in range(2))
    top, bottom = block[:H], block[H:]
    diagonal = jnp.sum(jnp.where(lane == row + H, bottom, 0.0), axis=0, keepdims=True)
    return jnp.where((lane < H) & (row > lane), pltpu.roll(bottom, H, 1), top), diagonal


def unpacked(half, diagonal):
    row, lane = (lax.broadcasted_iota(jnp.int32, (H, N), d) for d in range(2))
    turned = jnp.concatenate([half, jnp.zeros((H, N), jnp.float32)], axis=0).T
    top = jnp.where((lane < H) & (row > lane), turned[:H], half)
    upper = jnp.where(row == lane - H, jnp.broadcast_to(diagonal, (H, N)), pltpu.roll(turned[:H], H, 1))
    return top, jnp.where(lane < H, turned[H:], jnp.where(row > lane - H, pltpu.roll(half, H, 1), upper))


def pack_kernel(pattern, retained, parity, density, up, down, far, near):
    def find(x, code):
        slot = jnp.int32(-1)
        for t in range(SLOTS):
            slot = jnp.where(pattern[0, x, t] == code, SLOTS * x + t, slot)
        return slot

    def place(slot, targets):
        block = density[rows_of(jnp.maximum(slot, 0)), :] * (slot >= 0).astype(jnp.float32)
        for ref, first in targets:
            ref[pl.ds(first, N), :] = block

    par = parity[0]
    edges = TILE + 2 * H
    for i, (x, code) in enumerate(((0, 5), (0, 3), (1, 5))):
        place(find(x, code), ((up, edges + i * N), (down, edges + i * N)))
    place(find(0, 0), ((up, edges + 3 * N),))
    place(find(1, 2), ((up, edges + 4 * N),))
    place(find(0, 6), ((down, edges + 3 * N),))
    place(find(1, 8), ((down, edges + 4 * N),))
    far_half, far_diagonal = packed(density[rows_of(SLOTS * par), :])
    near_half, near_diagonal = packed(density[rows_of(SLOTS * (1 - par)), :])
    far_tile = code_tile(retained, par)
    near_tile = code_tile(retained, 1 - par)
    row = lax.broadcasted_iota(jnp.int32, (TILE, N), 0)
    tile = jnp.where(row == 0, near_tile + pltpu.roll(far_tile, SLOTS, 1), 0.0)
    tile = jnp.where(row == 1, near_diagonal, jnp.where(row == 2, far_diagonal, tile))
    for ref in (up, down):
        ref[pl.ds(0, TILE), :] = tile
        ref[pl.ds(TILE, H), :] = near_half
        ref[pl.ds(TILE + H, H), :] = far_half
    sides = ((far, par, far_tile, far_diagonal, far_half, (7,)), (near, 1 - par, near_tile, near_diagonal, near_half, (1, 7)))
    for ref, x, tile, diagonal, half, codes in sides:
        ref[pl.ds(0, TILE), :] = jnp.where(row == 1, diagonal, tile)
        ref[pl.ds(TILE, H), :] = half
        for i, code in enumerate(codes):
            place(find(x, code), ((ref, SELF + i * N),))


def step1_kernel(
    pattern, retained, parity, table, density, below, above, far, rel_below, rel_above, near_all,
    rows_out, far_out, codes_out, buf, heads, codes, out, lookup, used, ghigh, glow, sems, out_sems, table_sem,
):
    par = parity[0]
    table_copy = pltpu.make_async_copy(table, lookup, table_sem)
    table_copy.start()
    edges = TILE + 2 * H
    moves = [
        (density, 0, OWN, 8), (below, edges, BELOW + 2, 5), (above, edges, ABOVE + 2, 5),
        (far, SELF, LEFT + 2 + 3 * par, 1), (near_all, SELF, RIGHT + 1 - 3 * par, 2),
        (rel_above, SELF, T0 + LEFT + 1 + 3 * par, 1),
    ]
    parts = [
        (below, 0, edges, ((BELOW + 1 - par, TILE, 1), (BELOW + par, SELF, 2))),
        (above, 0, edges, ((ABOVE + 1 - par, TILE, 1), (ABOVE + par, SELF, 2))),
        (far, 0, SELF, ((LEFT + 3 * par, TILE, 1),)),
        (near_all, 0, SELF, ((RIGHT - 3 * par, TILE, 1),)),
        (rel_below, 0, SELF, ((CORNER + par, TILE, 1),)),
        (rel_above, 0, SELF, ((CORNER + 2 + par, TILE, 1),)),
        (near_all, HROWS, SELF, ((CORNER + 1 - par, TILE, 1),)),
        (near_all, HROWS + SELF, SELF, ((CORNER + 3 - par, TILE, 1),)),
    ]
    copies = []
    for i, (src, first, block, count) in enumerate(moves):
        copy = pltpu.make_async_copy(src.at[pl.ds(first, count * N), :], buf.at[rows_of(block, count), :], sems.at[i])
        copy.start()
        copies.append(copy)
    at, halves_at, tiles_at = 0, [], []
    for i, (src, first, count, selves) in enumerate(parts):
        copy = pltpu.make_async_copy(src.at[pl.ds(first, count), :], heads.at[pl.ds(at, count), :], sems.at[len(moves) + i])
        copy.start()
        copies.append(copy)
        halves_at += [(block, at + half, at + diagonal) for block, half, diagonal in selves]
        tiles_at.append(at)
        at += count

    table_copy.wait()
    for x in range(2):
        for t in range(SLOTS):
            code = pattern[0, x, t]
            a, b = offset(code)
            there = 5 + x + 4 * a + b
            block = SLOTS * x + t
            lookup[there * 9 + 8 - code] = block if t == 0 else T0 + block
    for x in range(2):
        for t in range(SLOTS):
            lookup[(5 + x) * 9 + pattern[0, x, t]] = SLOTS * x + t
    for block in range(STEP1_BLOCKS):
        used[block] = 0

    def find(x, lefts):
        places = []
        for s in range(SLOTS):
            left = lefts[0, x, s]
            a, b = offset(left)
            y = 5 + x + 4 * a + b
            for u in range(SLOTS):
                code, there = relative(left, retained[0, x, u])
                where = jnp.where(there, lookup[jnp.where(there, y * 9 + code, 0)], ZERO)
                used[where] = 1
                places.append((where, s, u))
        return places

    places = [(find(x, pattern), find(x, retained)) for x in range(2)]
    buf[rows_of(ZERO), :] = jnp.zeros((N, N), jnp.float32)
    for copy in copies:
        copy.wait()
    row = lax.broadcasted_iota(jnp.int32, (TILE, N), 0)
    tile = jnp.zeros((TILE, N), jnp.float32)
    for i, at in enumerate(tiles_at):
        tile = jnp.where(row == i, jnp.broadcast_to(heads[pl.ds(at, 1), :], (TILE, N)), tile)
    codes[...] = tile
    def unpack(block, half, diagonal):
        @pl.when(used[block] == 1)
        def _():
            top, bottom = unpacked(heads[pl.ds(half, H), :], heads[pl.ds(diagonal, 1), :])
            buf[rows_of(block), :] = jnp.concatenate([top, bottom], axis=0)

    def turn(block, other):
        @pl.when(used[other] == 1)
        def _():
            buf[rows_of(other), :] = buf[rows_of(block), :].T

    for args in halves_at:
        unpack(*args)
    far_up, near_up = LEFT + 1 + 3 * par, RIGHT + 1 - 3 * par
    turned = [(block, T0 + block) for block in (*TURNED, far_up + 1, near_up, near_up + 1)] + [(T0 + far_up, far_up)]
    for block, other in turned:
        turn(block, other)

    def gather(chosen):
        for where, s, u in chosen:
            put_factor(buf, where, ghigh, glow, s, u)

    for x in range(2):
        gather(places[x][0])
        left = jnp.concatenate([buf[rows_of(SLOTS * x + s), :] for s in range(SLOTS)], axis=1)
        square = times(left, ghigh, glow)
        gather(places[x][1])
        result = 3.0 * square - 2.0 * times(square, ghigh, glow)
        pos = lax.rem(par + x, 2)
        for u in range(SLOTS):
            out[rows_of(SLOTS * pos + u), :] = result[:, u * N : (u + 1) * N]
    ends = []
    for i, (src, ref) in enumerate(((out.at[pl.ds(0, 4 * N), :], far_out), (out, rows_out), (codes, codes_out))):
        copy = pltpu.make_async_copy(src, ref, out_sems.at[i])
        copy.start()
        ends.append(copy)
    for copy in ends:
        copy.wait()


def start(copies, src, dst, sems):
    copy = pltpu.make_async_copy(src, dst, sems.at[len(copies)])
    copy.start()
    copies.append(copy)


def finish(copies):
    for copy in copies:
        copy.wait()


def step2_kernel(side, retained, parity, table, codes_in, own, below, above, *refs):
    par = parity[0]
    moves = [(own, 0, 8), (below, 8, 8), (above, 16, 8)]
    if side == "far":
        x = par
        moves += [(refs[0], 24, 4), (refs[1], 32, 4), (refs[2], 36, 4)]
        result_out = refs[3]
    else:
        x = 1 - par
        moves += [(refs[0], 40, 12)]
        far_result, result_out = refs[1:3]
    codes, buf, out, ghigh, glow, sems, out_sems = refs[-7:]
    copies, written = [], []
    start(copies, codes_in, codes.at[pl.ds(0, TILE), :], sems)
    for src, block, count in moves:
        start(copies, src, buf.at[rows_of(block, count), :], sems)
    if side == "near":
        start(written, far_result, result_out.at[rows_of(SLOTS * par, SLOTS), :], out_sems)
    for t in range(2 * SLOTS):
        codes[TILE, t] = retained[0, t // SLOTS, t % SLOTS].astype(jnp.float32)
    buf[rows_of(STEP2_ZERO), :] = jnp.zeros((N, N), jnp.float32)
    copies[0].wait()
    places = []
    for s in range(SLOTS):
        left = retained[0, x, s]
        a, b = offset(left)
        entry = (par * 12 + 5 + x + 4 * a + b) * 3
        theirs = [codes[table[entry], table[entry + 1] + t].astype(jnp.int32) for t in range(SLOTS)]
        first_block = table[entry + 2]
        for u in range(SLOTS):
            code, there = relative(left, retained[0, x, u])
            where = jnp.int32(STEP2_ZERO)
            for t in range(SLOTS):
                where = jnp.where(there & (theirs[t] == code), first_block + t, where)
            places.append((where, s, u))
    finish(copies[1:])
    for where, s, u in places:
        put_factor(buf, where, ghigh, glow, s, u)
    mine = 0 if side == "far" else SLOTS
    left = jnp.concatenate([buf[rows_of(mine + s), :] for s in range(SLOTS)], axis=1)
    square = times(left, ghigh, glow)
    result = times(3.0 * left - 2.0 * square, ghigh, glow)
    for u in range(SLOTS):
        out[rows_of(u), :] = result[:, u * N : (u + 1) * N]
    if side == "near":
        start(written, out, result_out.at[rows_of(SLOTS * x, SLOTS), :], out_sems)
    else:
        start(written, out, result_out, out_sems)
    finish(written)


SMEM = pl.BlockSpec(memory_space=pltpu.SMEM)
VMEM = pl.BlockSpec(memory_space=pltpu.VMEM)
ANY = pl.BlockSpec(memory_space=pl.ANY)
COST = pl.CostEstimate(flops=10**11, bytes_accessed=10**8, transcendentals=0)
HBM = pl.BlockSpec(memory_space=pltpu.HBM)
PARAMS = pltpu.CompilerParams(vmem_limit_bytes=40 * 2**20)


FACTOR = [pltpu.VMEM((4 * N, 4 * N), jnp.bfloat16)] * 2


def step2(side, out_rows, *args):
    return pl.pallas_call(
        functools.partial(step2_kernel, side),
        out_shape=rows(out_rows),
        in_specs=[SMEM] * 3 + [ANY] * (len(args) - 2),
        out_specs=ANY,
        scratch_shapes=[
            pltpu.SMEM((TILE + 1, N), jnp.float32),
            pltpu.VMEM((STEP2_BLOCKS * N, N), jnp.float32),
            pltpu.VMEM((4 * N, N), jnp.float32),
            *FACTOR,
            pltpu.SemaphoreType.DMA((7,)),
            pltpu.SemaphoreType.DMA((2,)),
        ],
        compiler_params=PARAMS,
    )(*args[:2], jnp.asarray(FAR_TABLE.reshape(-1)), *args[2:])


def rows(count):
    return jax.ShapeDtypeStruct((count, N), jnp.float32)


def send(x, target):
    count_a, count_b = lax.axis_size("row"), lax.axis_size("col")
    pairs = []
    for a in range(count_a):
        for b in range(count_b):
            to_a, to_b = target(a, b)
            pairs.append((a * count_b + b, (to_a % count_a) * count_b + to_b % count_b))
    return lax.ppermute(x, ("row", "col"), pairs)


def to_above(x):
    return send(x, lambda a, b: (a - 1, b))


def to_below(x):
    return send(x, lambda a, b: (a + 1, b))


def far_side(b):
    return b + 1 if b % 2 else b - 1


def corner_to_above(x):
    return send(x, lambda a, b: (a - 1, b if a % GROUP else far_side(b)))


def corner_to_below(x):
    return send(x, lambda a, b: (a + 1, b if (a + 1) % GROUP else far_side(b)))


def to_far(x):
    return send(x, lambda a, b: (a, far_side(b)))


def to_near(x):
    return send(x, lambda a, b: (a, b ^ 1))


def corner_kernel(row, mine, theirs, to_above, to_below):
    line = lax.rem(row[0], GROUP)
    for there, out in ((0, to_above), (GROUP - 1, to_below)):
        part = pl.ds(0, out.shape[0])

        @pl.when(line == there)
        def _():
            out[...] = mine[part, :]

        @pl.when(line != there)
        def _():
            out[...] = theirs[part, :]


def corners(mine, theirs, above_rows):
    to_above, to_below = pl.pallas_call(
        corner_kernel,
        out_shape=(rows(above_rows), rows(mine.shape[0])),
        in_specs=[SMEM, VMEM, VMEM],
        out_specs=(VMEM, VMEM),
        compiler_params=PARAMS,
        cost_estimate=COST,
    )(jnp.full((1,), lax.axis_index("row"), jnp.int32), mine, theirs)
    return corner_to_above(to_above), corner_to_below(to_below)


def on_device(density, pattern, retained):
    shape = density.shape
    density = density.reshape(-1, N)
    parity = jnp.full((1,), lax.axis_index("col") % 2, jnp.int32)

    up, down, far_sent, near = pl.pallas_call(
        pack_kernel,
        out_shape=(rows(VROWS), rows(VROWS), rows(FROWS), rows(HROWS)),
        in_specs=[SMEM, SMEM, SMEM, VMEM],
        out_specs=(VMEM,) * 4,
        compiler_params=PARAMS,
    )(pattern, retained, parity, density)
    far = to_far(far_sent)
    below = to_above(up)
    above = to_below(down)
    rel_below, rel_above = corners(far_sent, far, SELF)
    below, above, rel_below, rel_above = lax.optimization_barrier((below, above, rel_below, rel_above))
    near_all = to_near(jnp.concatenate([near, below[:SELF], above[:SELF]]))

    own_rows, far_rows, codes = pl.pallas_call(
        step1_kernel,
        out_shape=(rows(8 * N), rows(4 * N), rows(TILE)),
        in_specs=[SMEM] * 3 + [ANY] * 8,
        out_specs=(HBM,) * 3,
        scratch_shapes=[
            pltpu.VMEM((STEP1_BLOCKS * N, N), jnp.float32),
            pltpu.VMEM((2 * (TILE + 2 * H) + 6 * SELF, N), jnp.float32),
            pltpu.VMEM((TILE, N), jnp.float32),
            pltpu.VMEM((8 * N, N), jnp.float32),
            pltpu.SMEM((108,), jnp.int32),
            pltpu.SMEM((STEP1_BLOCKS,), jnp.int32),
            pltpu.VMEM((4 * N, 4 * N), jnp.bfloat16),
            pltpu.VMEM((4 * N, 4 * N), jnp.bfloat16),
            pltpu.SemaphoreType.DMA((14,)),
            pltpu.SemaphoreType.DMA((3,)),
            pltpu.SemaphoreType.DMA,
        ],
        compiler_params=PARAMS,
    )(pattern, retained, parity, jnp.asarray(ring_table()), density, below, above, far, rel_below, rel_above, near_all)

    far = to_far(far_rows)
    below = to_above(own_rows)
    above = to_below(own_rows)
    far_below, far_above = corners(far_rows, far, 4 * N)
    below, above, far_below, far_above = lax.optimization_barrier((below, above, far_below, far_above))
    near_all = to_near(jnp.concatenate([above[4 * N :], below[4 * N :], own_rows[4 * N :]]))
    shared = (retained, parity, codes, own_rows, below, above)
    result = step2("far", 4 * N, *shared, far, far_below, far_above)
    result = step2("near", 8 * N, *shared, near_all, result)
    return result.reshape(shape)


def solution(mesh):
    return jax.shard_map(
        on_device,
        mesh=mesh,
        in_specs=(P("row", "col", None, None, None), P("row", "col", None), P("row", "col", None)),
        out_specs=P("row", "col", None, None, None),
        check_vma=False,
    )
```
